256 devices in a mesh: dp: 64 (over y, z, x_hi), seq: 4 (over x_lo, core).
Axes of the slice: x: 4 (x_hi: 2, x_lo: 2; x = x_hi * 2 + x_lo), y: 4, z: 8, core: 2. Of those that a mesh axis runs over, the one named last changes fastest.
Arguments:
- layer_inputs: bfloat16 [65536, 4096], P(('dp', 'seq')), may hold values from -6 to 6
- output_grads: bfloat16 [65536, 14336], P(('dp', 'seq')), may hold values from -6 to 6
- query_inputs: bfloat16 [64, 8, 4096], P('dp', None, 'seq'), may hold values from -0.09375 to 0.09375
- query_grads: bfloat16 [64, 8, 14336], P('dp', None, 'seq'), may hold values from -0.046875 to 0.046875
- input_eigen: float32 [4096], P('seq'), may hold values from 0.1 to 3
- output_eigen: float32 [14336], P('seq'), may hold values from 0.1 to 3
- doc_index: int32 [64, 1024], P('dp', 'seq'), may hold values from 0 to 7, never falling along the last dimension, each value on 1 to 256 neighbouring positions
- kept_counts: int32 [64, 8], P('dp'), may hold values from 1 to 256
Outputs:
- influence: float32 [64, 512], P('seq', 'dp')
The draws below stay inside these ranges and needn't reach their ends.
Inputs may be any that keep to these rules, and one draw needn't show every extreme that they name: `doc_index`: in each row document numbers never fall, every document 0 to 7 holds 1 to 256 tokens, and some document holds exactly 256.
All inputs are finite; a program needn't handle non-finite values.
Results may differ from the reference program's by a relative error of at most 0.0041.
Values may be sent and summed in bfloat16 or wider, within the bound.
No kernel may reach another device: no remote copies, remote signals or barrier semaphores. Data moves between devices by JAX's collectives and lax.ppermute only.
A program may use at most 128 MiB of HBM per device.

```python
import math
import jax
import jax.numpy as jnp
import numpy as np
from jax import lax

D = 4096
FF = 14336
RANK = 8
DOCS = 8
SEQ = 1024
MOST = 256
QUERIES = 64
TOKENS = 65536
N_DP = 64


def place_ends(values, rng, low, high):
    index_at = [jax.random.randint(jax.random.fold_in(rng, axis), (), 0, length) for axis, length in enumerate(values.shape)]
    longest = values.shape.index(max(values.shape))
    next_to = index_at[:longest] + [(index_at[longest] + 1) % values.shape[longest]] + index_at[longest + 1:]
    return values.at[tuple(index_at)].set(low).at[tuple(next_to)].set(high)


def levels(stream_key, shape, cuts, low, largest):
    gain = 1.0
    for axis_at, shards_of in cuts:
        heights = jax.random.uniform(jax.random.fold_in(jax.random.fold_in(stream_key, 6), axis_at), (shards_of,), jnp.float32, low / len(cuts), largest / len(cuts))
        gain = gain * jnp.repeat(jnp.exp(heights), shape[axis_at] // shards_of).reshape((-1,) + (1,) * (len(shape) - 1 - axis_at))
    return gain


def profile(number_of, total, most, skew):
    weights = [(1 << 20) // math.isqrt(grade ** skew) + 1 for grade in range(2, number_of + 1)]
    rest, given = total - most - (number_of - 1), [1] * (number_of - 1)
    while rest > 0:
        free = [i for i in range(number_of - 1) if given[i] < most]
        mass, remaining = sum([weights[i] for i in free]), rest
        for i in free:
            extra = min(most - given[i], max(1, remaining * weights[i] // mass), rest)
            given[i] = given[i] + extra
            rest = rest - extra
    return np.array([most] + given)


def ragged(key, count, total, reach, skew):
    if count == 2:
        one = jax.random.randint(key, (), max(1, total - reach), min(reach, total - 1) + 1)
        return jnp.stack([one, total - one])
    sizes = jnp.asarray(profile(count, total, reach, skew), jnp.int32)
    pairs = (count - 1) // 2
    donor, receiver = sizes[1:1 + 2 * pairs:2], sizes[2:2 + 2 * pairs:2]
    room = jnp.minimum(donor - 1, reach - receiver)
    passed = jax.random.randint(jax.random.fold_in(key, 1), (pairs,), 0, 1 << 20) % (room + 1)
    sizes = sizes.at[1:1 + 2 * pairs:2].set(donor - passed).at[2:2 + 2 * pairs:2].set(receiver + passed)
    return sizes[jax.random.permutation(jax.random.fold_in(key, 2), count)]


def scatter_about(stream_key, shape, width, most, cuts=(), held_as=jnp.bfloat16):
    entries = width * jax.random.normal(stream_key, shape, jnp.float32)
    if cuts:
        entries = entries * levels(stream_key, shape, cuts, -0.22, 0.18)
    return jnp.clip(entries, -most, most).astype(held_as)


def setup_inputs(seed: int = 0) -> dict:
    arg_keys = jax.random.split(jax.random.key(seed), 9)
    return {
        "layer_inputs": scatter_about(arg_keys[0], (TOKENS, D), 1.0, 6.0, ((0, 256),)),
        "output_grads": scatter_about(arg_keys[1], (TOKENS, FF), 1.0, 6.0, ((0, 256),)),
        "query_inputs": scatter_about(arg_keys[2], (QUERIES, RANK, D), D ** -0.5, 0.09375, ((0, 64), (2, 4))),
        "query_grads": scatter_about(arg_keys[3], (QUERIES, RANK, FF), FF ** -0.5, 0.046875, ((0, 64), (2, 4))),
        "input_eigen": jnp.clip(jnp.exp(math.log(3.0) - 3.4011974 * jax.random.uniform(arg_keys[4], (D,), jnp.float32) ** levels(arg_keys[4], (D,), ((0, 4),), -0.2, 0.2)), 0.1, 3.0),
        "output_eigen": jnp.clip(jnp.exp(math.log(3.0) - 3.4011974 * jax.random.uniform(arg_keys[5], (FF,), jnp.float32) ** levels(arg_keys[5], (FF,), ((0, 4),), -0.2, 0.2)), 0.1, 3.0),
        "doc_index": jax.vmap(lambda own: jnp.searchsorted(jnp.cumsum(ragged(own, DOCS, SEQ, MOST, 1)), jnp.arange(SEQ), side="right"))(jax.random.split(arg_keys[6], N_DP)).reshape((N_DP, SEQ)).astype(jnp.int32),
        "kept_counts": place_ends(jax.random.randint(arg_keys[7], (N_DP, DOCS), 1, MOST + 1), jax.random.fold_in(arg_keys[7], 1), 1, MOST).astype(jnp.int32),
    }


damping = 0.1

def doc_weights(row_ids, row_kept):
    positions = jnp.arange(row_ids.shape[0], dtype=jnp.int32)
    onehot = (row_ids[:, None] == jnp.arange(DOCS, dtype=jnp.int32)[None, :]).astype(jnp.int32)
    length = lax.optimization_barrier(jnp.sum(onehot, axis=0)).astype(jnp.int32)
    first = (jnp.cumsum(length) - length).astype(jnp.int32)
    offset = positions - lax.optimization_barrier(jnp.sum(onehot * first[None, :], axis=1))
    limit = lax.optimization_barrier(jnp.sum(onehot * row_kept[None, :], axis=1))
    used = jnp.minimum(length, row_kept).astype(jnp.float32)
    counted = (offset < limit).astype(jnp.float32)
    return onehot.astype(jnp.float32) * counted[:, None] / jnp.sqrt(used)[None, :]

def reference(layer_inputs, output_grads, query_inputs, query_grads, input_eigen, output_eigen, doc_index, kept_counts):
    pre_in = (query_inputs.astype(jnp.float32) / (input_eigen + damping)[None, None, :]).astype(jnp.bfloat16)
    pre_out = (query_grads.astype(jnp.float32) / (output_eigen + damping)[None, None, :]).astype(jnp.bfloat16)
    pre_in = pre_in.reshape(QUERIES * RANK, D)
    pre_out = pre_out.reshape(QUERIES * RANK, FF)
    rows_in = layer_inputs.reshape(N_DP, SEQ, D)
    rows_out = output_grads.reshape(N_DP, SEQ, FF)

    def one_row(packed):
        row_in, row_out, row_ids, row_kept = packed
        in_proj = jnp.dot(row_in, pre_in.T, preferred_element_type=jnp.float32)
        out_proj = jnp.dot(row_out, pre_out.T, preferred_element_type=jnp.float32)
        token_score = lax.optimization_barrier(jnp.sum((in_proj * out_proj).reshape(SEQ, QUERIES, RANK), axis=2))
        weights = doc_weights(row_ids, row_kept)
        return jnp.dot(token_score.T, weights, precision=lax.Precision.HIGHEST)
    per_row = lax.map(one_row, (rows_in, rows_out, doc_index, kept_counts))
    return jnp.transpose(per_row, (1, 0, 2)).reshape(QUERIES, N_DP * DOCS)
```

```python
import functools

import jax
import jax.numpy as jnp
from jax import lax
from jax.experimental import pallas as pl
from jax.experimental.pallas import tpu as pltpu
from jax.sharding import Mesh
from jax.sharding import PartitionSpec as P

RANK = 8
DOCS = 8
NY, NZ, NX = 4, 8, 4
AXES = ("y", "z", "xh", "xl", "core")
SIZE = {"y": NY, "z": NZ, "x": NX}
damping = 0.1

ROWS = 256
HALF_IN, HALF_OUT = 512, 1792
CHUNK = HALF_IN + HALF_OUT
NT = (((1,), (1,)), ((), ()))


def device_at(y, z, x, core):
    return ((y * NZ + z) * NX + x) * 2 + core


def shift(value, axis, step0, step1):
    pairs = []
    for y in range(NY):
        for z in range(NZ):
            for x in range(NX):
                for core in range(2):
                    at = {"y": y, "z": z, "x": x}
                    at[axis] = (at[axis] + (step1 if core else step0)) % SIZE[axis]
                    pairs.append((device_at(y, z, x, core), device_at(at["y"], at["z"], at["x"], core)))
    return lax.ppermute(value, AXES, pairs)


def swap_cores(value):
    return lax.ppermute(value, "core", [(0, 1), (1, 0)])


def direct(own, axis):
    return [own, shift(own, axis, 1, -1), shift(own, axis, 2, -2), shift(own, axis, -1, 1)]


def gather_z(own):
    a = shift(own, "z", 1, -1)
    b = shift(own, "z", -1, 1)
    a2 = shift(own, "z", 2, -2)
    b2 = shift(own, "z", -2, 2)
    c = shift(jnp.concatenate([a, a2], axis=0), "z", 2, -2)
    d = shift(b, "z", -2, 2)
    return jnp.concatenate([own, a, a2, c, d, b2, b], axis=0), a


def doc_weights(row_ids, row_kept):
    positions = jnp.arange(row_ids.shape[0], dtype=jnp.int32)
    onehot = (row_ids[None, :] == jnp.arange(DOCS, dtype=jnp.int32)[:, None]).astype(jnp.int32)
    length = jnp.sum(onehot, axis=1)
    first = jnp.cumsum(length) - length
    used = jnp.minimum(length, row_kept).astype(jnp.float32)
    counted = (positions[None, :] - first[:, None] < row_kept[:, None]).astype(jnp.float32)
    return onehot.astype(jnp.float32) * counted / jnp.sqrt(used)[:, None]


def project(odd, where, tokens, first, second, acc_in, acc_out, xs, gs, ws, sems):
    def copies(piece):
        half, quarter = divmod(piece, 2)
        at = (where[3] ^ odd) * 4 + quarter * 2 + half
        of_x = pl.ds(pl.multiple_of(at * HALF_IN, 128), HALF_IN)
        of_g = pl.ds(pl.multiple_of(at * HALF_OUT, 128), HALF_OUT)
        of_w = pl.ds(quarter * CHUNK, CHUNK)
        x_own, x_other, g_own, g_other = tokens
        moves = [
            (x_own.at[:, of_x], xs.at[piece, pl.ds(0, 256)]),
            (x_other.at[:, of_x], xs.at[piece, pl.ds(256, 256)]),
            (g_own.at[:, of_g], gs.at[piece, pl.ds(0, 256)]),
            (g_other.at[:, of_g], gs.at[piece, pl.ds(256, 256)]),
        ]
        if half == 0:
            moves += [(v.at[:, of_w], ws.at[piece, pl.ds(64 * i, 64)]) for i, v in enumerate(first)]
        else:
            moves += [
                (second[y].at[pl.ds(32 * k, 32), of_w], ws.at[piece, pl.ds(128 * k + 32 * y, 32)])
                for k in range(2)
                for y in range(4)
            ]
        return [pltpu.make_async_copy(src, dst, sems.at[piece, i]) for i, (src, dst) in enumerate(moves)]

    for piece in range(4):
        for copy in copies(piece):
            copy.start()
    for piece in range(4):
        for copy in copies(piece):
            copy.wait()
        p = lax.dot_general(xs[piece], ws[piece, :, :HALF_IN], NT, preferred_element_type=jnp.float32)
        q = lax.dot_general(gs[piece], ws[piece, :, HALF_IN:], NT, preferred_element_type=jnp.float32)
        if piece == 0:
            acc_in[...] = p
            acc_out[...] = q
        else:
            acc_in[...] += p
            acc_out[...] += q


def even_kernel(where, *refs):
    project(0, where, refs[:4], refs[4:8], refs[8:12], *refs[12:])


def odd_kernel(where, *refs):
    w_own, w_other, even_in, even_out = refs[12:16]
    outs, (acc_in, acc_out, *scratch) = refs[16:20], refs[20:]
    project(1, where, refs[:4], refs[4:8], refs[8:12], acc_in, acc_out, *scratch)
    y, z, xh, xl, core = (where[i] for i in range(5))
    swapped = xl == core

    def total(even, acc):
        odd = acc[...]
        turned = jnp.concatenate([odd[:, 128:], odd[:, :128]], axis=1)
        return even[...] + jnp.where(swapped, turned, odd)

    prod = total(even_in, acc_in) * total(even_out, acc_out)
    weights = jnp.concatenate([w_own[...], w_other[...]], axis=1)
    sums = jnp.dot(weights, prod, precision=lax.Precision.HIGHEST, preferred_element_type=jnp.float32)
    row = lax.broadcasted_iota(jnp.int32, (16, ROWS), 1)
    slot = lax.broadcasted_iota(jnp.int32, (16, ROWS), 0)
    sign = 2 * core - 1
    row_z = (z + sign * ((row >> 2) & 7)) & 7
    row_y = (y + sign * ((row >> 5) & 3)) & 3
    row_xh = xh ^ (row >> 7)
    row_query = (row_y * 8 + row_z) * 2 + row_xh
    seq = xl * 2 + core
    for away in range(4):
        pick = (row_query == (seq ^ away) * 16 + slot).astype(jnp.float32)
        outs[away][...] = lax.dot_general(
            sums, pick, NT, precision=lax.Precision.HIGHEST, preferred_element_type=jnp.float32
        )


def score(where, tokens, first, second, extra=()):
    last = bool(extra)
    proj = (512, ROWS)
    vmem = pl.BlockSpec(memory_space=pltpu.VMEM)
    shapes = [(DOCS, 16)] * 4 if last else [proj] * 2
    return pl.pallas_call(
        odd_kernel if last else even_kernel,
        in_specs=[pl.BlockSpec(memory_space=pltpu.SMEM)]
        + [pl.BlockSpec(memory_space=pl.ANY)] * 12
        + [vmem] * len(extra),
        out_specs=[vmem] * len(shapes),
        out_shape=[jax.ShapeDtypeStruct(shape, jnp.float32) for shape in shapes],
        scratch_shapes=([pltpu.VMEM(proj, jnp.float32)] * 2 if last else [])
        + [
            pltpu.VMEM((4, 512, HALF_IN), jnp.bfloat16),
            pltpu.VMEM((4, 512, HALF_OUT), jnp.bfloat16),
            pltpu.VMEM((4, ROWS, CHUNK), jnp.bfloat16),
            pltpu.SemaphoreType.DMA((4, 12)),
        ],
        compiler_params=pltpu.CompilerParams(vmem_limit_bytes=60 * 1024 * 1024),
        cost_estimate=pl.CostEstimate(
            flops=2 * 512 * ROWS * 4 * CHUNK, bytes_accessed=2 * 768 * 4 * CHUNK, transcendentals=0
        ),
    )(where, *tokens, *first, *second, *extra)


def shards(
    layer_inputs,
    output_grads,
    query_inputs,
    query_grads,
    input_eigen,
    output_eigen,
    doc_index,
    kept_counts,
):
    y, z, xh, xl, core = (lax.axis_index(a) for a in AXES)
    pre_in = (query_inputs[0].astype(jnp.float32) / (input_eigen + damping)[None, :]).astype(jnp.bfloat16)
    pre_out = (query_grads[0].astype(jnp.float32) / (output_eigen + damping)[None, :]).astype(jnp.bfloat16)
    pre = jnp.concatenate(
        [pre_in[:, :HALF_IN], pre_out[:, :HALF_OUT], pre_in[:, HALF_IN:], pre_out[:, HALF_OUT:]], axis=1
    )
    low, high = pre[:4], pre[4:]
    kept = jnp.where(core == 0, low, high)
    came = swap_cores(jnp.where(core == 0, high, low))
    both = jnp.where(core == 0, jnp.stack([kept, came], axis=1), jnp.stack([came, kept], axis=1))
    own = both.reshape(8, 2 * CHUNK)

    own, output_grads = lax.optimization_barrier((own, output_grads))
    g_other = swap_cores(output_grads)
    slots, first_came = gather_z(own)
    first_came, layer_inputs, own_ids = lax.optimization_barrier((first_came, layer_inputs, doc_index[0]))
    x_other = swap_cores(layer_inputs)
    ids = lax.all_gather(own_ids, ("xl", "core"), axis=0, tiled=True)

    halves = [slots[:, :CHUNK].reshape(32, 2 * CHUNK), slots[:, CHUNK:].reshape(32, 2 * CHUNK)]
    halves, x_other, g_other, ids = lax.optimization_barrier((halves, x_other, g_other, ids))

    first, second = direct(halves[0], "y"), direct(halves[1], "x")

    def go_round(one, two, axis):
        pair = [jnp.concatenate([one, two], axis=0)]
        for _ in range(3):
            pair.append(shift(pair[-1], axis, 1, -1))
        return pair

    even_second = go_round(second[0], second[2], "y")
    near_first = go_round(first[0], first[1], "x")
    far_first = go_round(first[2], first[3], "x")
    odd_second = go_round(second[1], second[3], "y")

    weights = doc_weights(ids, kept_counts[0])
    seq = xl * 2 + core
    w_own = lax.dynamic_slice(weights, (0, seq * 256), (DOCS, 256))
    w_other = lax.dynamic_slice(weights, (0, (seq ^ 1) * 256), (DOCS, 256))

    where = jnp.stack([y, z, xh, xl, core]).astype(jnp.int32)
    tokens = (layer_inputs, x_other, output_grads, g_other)
    even = score(where, tokens, [near_first[0], far_first[0], near_first[2], far_first[2]], even_second)
    pieces = score(
        where,
        tokens,
        [near_first[1], far_first[1], near_first[3], far_first[3]],
        odd_second,
        (w_own, w_other, *even),
    )
    total = pieces[0]
    for away in (1, 2, 3):
        total = total + lax.ppermute(pieces[away], ("xl", "core"), [(i, i ^ away) for i in range(4)])
    return total.T


def solution(mesh):
    fine = Mesh(mesh.devices.reshape(NY, NZ, 2, 2, 2), AXES)
    dp, seq = ("y", "z", "xh"), ("xl", "core")
    placed = (
        P(dp + seq, None),
        P(dp + seq, None),
        P(dp, None, seq),
        P(dp, None, seq),
        P(seq),
        P(seq),
        P(dp, seq),
        P(dp, None),
    )
    return jax.shard_map(shards, mesh=fine, in_specs=placed, out_specs=P(seq, dp), check_vma=False)
```

```python
import functools

import jax
import jax.numpy as jnp
from jax import lax
from jax.experimental import pallas as pl
from jax.experimental.pallas import tpu as pltpu
from jax.sharding import Mesh
from jax.sharding import PartitionSpec as P

RANK = 8
DOCS = 8
NY, NZ, NX = 4, 8, 4
AXES = ("y", "z", "xh", "xl", "core")
SIZE = {"y": NY, "z": NZ, "x": NX}
damping = 0.1

ROWS = 256
HALF_IN, HALF_OUT = 512, 1792
CHUNK = HALF_IN + HALF_OUT
NT = (((1,), (1,)), ((), ()))
LIMIT = 32 * 1024 * 1024


def device_at(y, z, x, core):
    return ((y * NZ + z) * NX + x) * 2 + core


def shift(value, axis, step0, step1):
    pairs = []
    for y in range(NY):
        for z in range(NZ):
            for x in range(NX):
                for core in range(2):
                    at = {"y": y, "z": z, "x": x}
                    at[axis] = (at[axis] + (step1 if core else step0)) % SIZE[axis]
                    pairs.append((device_at(y, z, x, core), device_at(at["y"], at["z"], at["x"], core)))
    return lax.ppermute(value, AXES, pairs)


def swap_cores(value):
    return lax.ppermute(value, "core", [(0, 1), (1, 0)])


def direct(own, axis):
    return [own, shift(own, axis, 1, -1), shift(own, axis, 2, -2), shift(own, axis, -1, 1)]


def gather_z(own):
    a = shift(own, "z", 1, -1)
    b = shift(own, "z", -1, 1)
    a2 = shift(own, "z", 2, -2)
    b2 = shift(own, "z", -2, 2)
    c = shift(jnp.concatenate([a, a2], axis=0), "z", 2, -2)
    d = shift(b, "z", -2, 2)
    return jnp.concatenate([own, a, a2, c, d, b2, b], axis=0), a


def doc_weights(row_ids, row_kept):
    positions = jnp.arange(row_ids.shape[0], dtype=jnp.int32)
    onehot = (row_ids[None, :] == jnp.arange(DOCS, dtype=jnp.int32)[:, None]).astype(jnp.int32)
    length = jnp.sum(onehot, axis=1)
    first = jnp.cumsum(length) - length
    used = jnp.minimum(length, row_kept).astype(jnp.float32)
    counted = (positions[None, :] - first[:, None] < row_kept[:, None]).astype(jnp.float32)
    return onehot.astype(jnp.float32) * counted / jnp.sqrt(used)[:, None]


def project(odd, where, tokens, first, second, acc_in, acc_out, xs, gs, ws, sems):
    def copies(piece):
        half, quarter = divmod(piece, 2)
        at = (where[3] ^ odd) * 4 + quarter * 2 + half
        of_x = pl.ds(pl.multiple_of(at * HALF_IN, 128), HALF_IN)
        of_g = pl.ds(pl.multiple_of(at * HALF_OUT, 128), HALF_OUT)
        of_w = pl.ds(quarter * CHUNK, CHUNK)
        x_own, x_other, g_own, g_other = tokens
        moves = [
            (x_own.at[:, of_x], xs.at[piece, pl.ds(0, 256)]),
            (x_other.at[:, of_x], xs.at[piece, pl.ds(256, 256)]),
            (g_own.at[:, of_g], gs.at[piece, pl.ds(0, 256)]),
            (g_other.at[:, of_g], gs.at[piece, pl.ds(256, 256)]),
        ]
        if half == 0:
            moves += [(v.at[:, of_w], ws.at[piece, pl.ds(64 * i, 64)]) for i, v in enumerate(first)]
        else:
            moves += [
                (second[y].at[pl.ds(32 * k, 32), of_w], ws.at[piece, pl.ds(128 * k + 32 * y, 32)])
                for k in range(2)
                for y in range(4)
            ]
        return [pltpu.make_async_copy(src, dst, sems.at[piece, i]) for i, (src, dst) in enumerate(moves)]

    for piece in range(4):
        for copy in copies(piece):
            copy.start()
    for piece in range(4):
        for copy in copies(piece):
            copy.wait()
        p = lax.dot_general(xs[piece], ws[piece, :, :HALF_IN], NT, preferred_element_type=jnp.float32)
        q = lax.dot_general(gs[piece], ws[piece, :, HALF_IN:], NT, preferred_element_type=jnp.float32)
        if piece == 0:
            acc_in[...] = p
            acc_out[...] = q
        else:
            acc_in[...] += p
            acc_out[...] += q


def even_kernel(where, *refs):
    project(0, where, refs[:4], refs[4:8], refs[8:12], *refs[12:])


def odd_kernel(where, *refs):
    w_own, w_other, even_in, even_out = refs[12:16]
    outs, (acc_in, acc_out, *scratch) = refs[16:20], refs[20:]
    project(1, where, refs[:4], refs[4:8], refs[8:12], acc_in, acc_out, *scratch)
    y, z, xh, xl, core = (where[i] for i in range(5))
    swapped = xl == core

    def total(even, acc):
        odd = acc[...]
        turned = jnp.concatenate([odd[:, 128:], odd[:, :128]], axis=1)
        return even[...] + jnp.where(swapped, turned, odd)

    prod = total(even_in, acc_in) * total(even_out, acc_out)
    weights = jnp.concatenate([w_own[...], w_other[...]], axis=1)
    sums = jnp.dot(weights, prod, precision=lax.Precision.HIGHEST, preferred_element_type=jnp.float32)
    row = lax.broadcasted_iota(jnp.int32, (16, ROWS), 1)
    slot = lax.broadcasted_iota(jnp.int32, (16, ROWS), 0)
    sign = 2 * core - 1
    row_z = (z + sign * ((row >> 2) & 7)) & 7
    row_y = (y + sign * ((row >> 5) & 3)) & 3
    row_xh = xh ^ (row >> 7)
    row_query = (row_y * 8 + row_z) * 2 + row_xh
    seq = xl * 2 + core
    for away in range(4):
        pick = (row_query == (seq ^ away) * 16 + slot).astype(jnp.float32)
        outs[away][...] = lax.dot_general(
            sums, pick, NT, precision=lax.Precision.HIGHEST, preferred_element_type=jnp.float32
        )


def score(where, tokens, first, second, extra=()):
    last = bool(extra)
    proj = (512, ROWS)
    vmem = pl.BlockSpec(memory_space=pltpu.VMEM)
    shapes = [(DOCS, 16)] * 4 if last else [proj] * 2
    return pl.pallas_call(
        odd_kernel if last else even_kernel,
        in_specs=[pl.BlockSpec(memory_space=pltpu.SMEM)]
        + [pl.BlockSpec(memory_space=pl.ANY)] * 12
        + [vmem] * len(extra),
        out_specs=[vmem] * len(shapes),
        out_shape=[jax.ShapeDtypeStruct(shape, jnp.float32) for shape in shapes],
        scratch_shapes=([pltpu.VMEM(proj, jnp.float32)] * 2 if last else [])
        + [
            pltpu.VMEM((4, 512, HALF_IN), jnp.bfloat16),
            pltpu.VMEM((4, 512, HALF_OUT), jnp.bfloat16),
            pltpu.VMEM((4, ROWS, CHUNK), jnp.bfloat16),
            pltpu.SemaphoreType.DMA((4, 12)),
        ],
        compiler_params=pltpu.CompilerParams(vmem_limit_bytes=LIMIT),
        cost_estimate=pl.CostEstimate(
            flops=2 * 512 * ROWS * 4 * CHUNK, bytes_accessed=2 * 768 * 4 * CHUNK, transcendentals=0
        ),
    )(where, *tokens, *first, *second, *extra)


def shards(
    layer_inputs,
    output_grads,
    query_inputs,
    query_grads,
    input_eigen,
    output_eigen,
    doc_index,
    kept_counts,
):
    y, z, xh, xl, core = (lax.axis_index(a) for a in AXES)
    pre_in = (query_inputs[0].astype(jnp.float32) / (input_eigen + damping)[None, :]).astype(jnp.bfloat16)
    pre_out = (query_grads[0].astype(jnp.float32) / (output_eigen + damping)[None, :]).astype(jnp.bfloat16)
    pre = jnp.concatenate(
        [pre_in[:, :HALF_IN], pre_out[:, :HALF_OUT], pre_in[:, HALF_IN:], pre_out[:, HALF_OUT:]], axis=1
    )
    low, high = pre[:4], pre[4:]
    kept = jnp.where(core == 0, low, high)
    came = swap_cores(jnp.where(core == 0, high, low))
    ids_came = swap_cores(doc_index[0])
    both = jnp.where(core == 0, jnp.stack([kept, came], axis=1), jnp.stack([came, kept], axis=1))
    own = both.reshape(8, 2 * CHUNK)

    chip_ids = jnp.where(core == 0, jnp.stack([doc_index[0], ids_came]), jnp.stack([ids_came, doc_index[0]]))
    own, output_grads, chip_ids = lax.optimization_barrier((own, output_grads, chip_ids))
    mate_ids = lax.ppermute(chip_ids, "xl", [(0, 1), (1, 0)])
    g_other = swap_cores(output_grads)
    slots, first_came = gather_z(own)
    first_came, layer_inputs, mate_ids = lax.optimization_barrier((first_came, layer_inputs, mate_ids))
    x_other = swap_cores(layer_inputs)

    halves = [slots[:, :CHUNK].reshape(32, 2 * CHUNK), slots[:, CHUNK:].reshape(32, 2 * CHUNK)]
    halves, x_other, g_other = lax.optimization_barrier((halves, x_other, g_other))

    first, second = direct(halves[0], "y"), direct(halves[1], "x")

    def go_round(one, two, axis):
        pair = [jnp.concatenate([one, two], axis=0)]
        for _ in range(3):
            pair.append(shift(pair[-1], axis, 1, -1))
        return pair

    even_second = go_round(second[0], second[2], "y")
    near_first = go_round(first[0], first[1], "x")
    far_first = go_round(first[2], first[3], "x")
    odd_second = go_round(second[1], second[3], "y")

    ids = jnp.where(xl == 0, jnp.stack([chip_ids, mate_ids]), jnp.stack([mate_ids, chip_ids])).reshape(-1)
    weights = doc_weights(ids, kept_counts[0])
    seq = xl * 2 + core
    w_own = lax.dynamic_slice(weights, (0, seq * 256), (DOCS, 256))
    w_other = lax.dynamic_slice(weights, (0, (seq ^ 1) * 256), (DOCS, 256))

    where = jnp.stack([y, z, xh, xl, core]).astype(jnp.int32)
    tokens = (layer_inputs, x_other, output_grads, g_other)
    even = score(where, tokens, [near_first[0], far_first[0], near_first[2], far_first[2]], even_second)
    pieces = score(
        where,
        tokens,
        [near_first[1], far_first[1], near_first[3], far_first[3]],
        odd_second,
        (w_own, w_other, *even),
    )
    total = pieces[0]
    for away in (1, 2, 3):
        total = total + lax.ppermute(pieces[away], ("xl", "core"), [(i, i ^ away) for i in range(4)])
    return total.T


def solution(mesh):
    fine = Mesh(mesh.devices.reshape(NY, NZ, 2, 2, 2), AXES)
    dp, seq = ("y", "z", "xh"), ("xl", "core")
    placed = (
        P(dp + seq, None),
        P(dp + seq, None),
        P(dp, None, seq),
        P(dp, None, seq),
        P(seq),
        P(seq),
        P(dp, seq),
        P(dp, None),
    )
    return jax.shard_map(shards, mesh=fine, in_specs=placed, out_specs=P(seq, dp), check_vma=False)
```

```python
import functools

import jax
import jax.numpy as jnp
from jax import lax
from jax.experimental import pallas as pl
from jax.experimental.pallas import tpu as pltpu
from jax.sharding import Mesh
from jax.sharding import PartitionSpec as P

RANK = 8
DOCS = 8
NY, NZ, NX = 4, 8, 4
AXES = ("y", "z", "xh", "xl", "core")
SIZE = {"y": NY, "z": NZ, "x": NX}
damping = 0.1

ROWS = 256
HALF_IN, HALF_OUT = 512, 1792
CHUNK = HALF_IN + HALF_OUT
NT = (((1,), (1,)), ((), ()))
LIMIT = 32 * 1024 * 1024


def device_at(y, z, x, core):
    return ((y * NZ + z) * NX + x) * 2 + core


def shift(value, axis, step0, step1):
    pairs = []
    for y in range(NY):
        for z in range(NZ):
            for x in range(NX):
                for core in range(2):
                    at = {"y": y, "z": z, "x": x}
                    at[axis] = (at[axis] + (step1 if core else step0)) % SIZE[axis]
                    pairs.append((device_at(y, z, x, core), device_at(at["y"], at["z"], at["x"], core)))
    return lax.ppermute(value, AXES, pairs)


def swap_cores(value):
    return lax.ppermute(value, "core", [(0, 1), (1, 0)])


def direct(own, axis):
    return [own, shift(own, axis, 1, -1), shift(own, axis, 2, -2), shift(own, axis, -1, 1)]


def gather_z(own):
    a = shift(own, "z", 1, -1)
    b = shift(own, "z", -1, 1)
    a2 = shift(own, "z", 2, -2)
    b2 = shift(own, "z", -2, 2)
    c = shift(jnp.concatenate([a, a2], axis=0), "z", 2, -2)
    d = shift(b, "z", -2, 2)
    return jnp.concatenate([own, a, a2, c, d, b2, b], axis=0), a


def doc_weights(row_ids, row_kept):
    positions = jnp.arange(row_ids.shape[0], dtype=jnp.int32)
    onehot = (row_ids[None, :] == jnp.arange(DOCS, dtype=jnp.int32)[:, None]).astype(jnp.int32)
    length = jnp.sum(onehot, axis=1)
    first = jnp.cumsum(length) - length
    used = jnp.minimum(length, row_kept).astype(jnp.float32)
    counted = (positions[None, :] - first[:, None] < row_kept[:, None]).astype(jnp.float32)
    return onehot.astype(jnp.float32) * counted / jnp.sqrt(used)[:, None]


def project(odd, where, tokens, first, second, acc_in, acc_out, xs, gs, ws, sems):
    def copies(piece):
        half, quarter = divmod(piece, 2)
        at = (where[3] ^ odd) * 4 + quarter * 2 + half
        of_x = pl.ds(pl.multiple_of(at * HALF_IN, 128), HALF_IN)
        of_g = pl.ds(pl.multiple_of(at * HALF_OUT, 128), HALF_OUT)
        of_w = pl.ds(quarter * CHUNK, CHUNK)
        x_own, x_other, g_own, g_other = tokens
        moves = [
            (x_own.at[:, of_x], xs.at[piece, pl.ds(0, 256)]),
            (x_other.at[:, of_x], xs.at[piece, pl.ds(256, 256)]),
            (g_own.at[:, of_g], gs.at[piece, pl.ds(0, 256)]),
            (g_other.at[:, of_g], gs.at[piece, pl.ds(256, 256)]),
        ]
        if half == 0:
            moves += [(v.at[:, of_w], ws.at[piece, pl.ds(64 * i, 64)]) for i, v in enumerate(first)]
        else:
            moves += [
                (second[y].at[pl.ds(32 * k, 32), of_w], ws.at[piece, pl.ds(128 * k + 32 * y, 32)])
                for k in range(2)
                for y in range(4)
            ]
        return [pltpu.make_async_copy(src, dst, sems.at[piece, i]) for i, (src, dst) in enumerate(moves)]

    for piece in range(4):
        for copy in copies(piece):
            copy.start()
    for piece in range(4):
        for copy in copies(piece):
            copy.wait()
        p = lax.dot_general(xs[piece], ws[piece, :, :HALF_IN], NT, preferred_element_type=jnp.float32)
        q = lax.dot_general(gs[piece], ws[piece, :, HALF_IN:], NT, preferred_element_type=jnp.float32)
        if piece == 0:
            acc_in[...] = p
            acc_out[...] = q
        else:
            acc_in[...] += p
            acc_out[...] += q


def even_kernel(where, *refs):
    project(0, where, refs[:4], refs[4:8], refs[8:12], *refs[12:])


def odd_kernel(where, *refs):
    w_own, w_other, even_in, even_out = refs[12:16]
    outs, (acc_in, acc_out, *scratch) = refs[16:20], refs[20:]
    project(1, where, refs[:4], refs[4:8], refs[8:12], acc_in, acc_out, *scratch)
    y, z, xh, xl, core = (where[i] for i in range(5))
    swapped = xl == core

    def total(even, acc):
        odd = acc[...]
        turned = jnp.concatenate([odd[:, 128:], odd[:, :128]], axis=1)
        return even[...] + jnp.where(swapped, turned, odd)

    prod = total(even_in, acc_in) * total(even_out, acc_out)
    own_prod, other_prod = prod[:256], prod[256:]
    by_doc = []
    for doc in range(DOCS):
        weighted = own_prod * w_own[:, doc : doc + 1] + other_prod * w_other[:, doc : doc + 1]
        by_doc.append(jnp.sum(weighted, axis=0, keepdims=True))
    sums = jnp.concatenate(by_doc, axis=0)
    row = lax.broadcasted_iota(jnp.int32, (64, ROWS), 1)
    slot = lax.broadcasted_iota(jnp.int32, (64, ROWS), 0)
    sign = 2 * core - 1
    row_z = (z + sign * ((row >> 2) & 7)) & 7
    row_y = (y + sign * ((row >> 5) & 3)) & 3
    row_xh = xh ^ (row >> 7)
    row_query = (row_y * 8 + row_z) * 2 + row_xh
    seq = xl * 2 + core
    pick = (row_query == (seq ^ (slot >> 4)) * 16 + (slot & 15)).astype(jnp.float32).astype(jnp.bfloat16)
    top = sums.astype(jnp.bfloat16)
    rest = sums - top.astype(jnp.float32)
    middle = rest.astype(jnp.bfloat16)
    low = (rest - middle.astype(jnp.float32)).astype(jnp.bfloat16)
    picked = sum(
        lax.dot_general(part, pick, NT, preferred_element_type=jnp.float32) for part in (low, middle, top)
    )
    for away in range(4):
        outs[away][...] = picked[:, 16 * away : 16 * away + 16]


def score(where, tokens, first, second, extra=()):
    last = bool(extra)
    proj = (512, ROWS)
    vmem = pl.BlockSpec(memory_space=pltpu.VMEM)
    shapes = [(DOCS, 16)] * 4 if last else [proj] * 2
    return pl.pallas_call(
        odd_kernel if last else even_kernel,
        in_specs=[pl.BlockSpec(memory_space=pltpu.SMEM)]
        + [pl.BlockSpec(memory_space=pl.ANY)] * 12
        + [vmem] * len(extra),
        out_specs=[vmem] * len(shapes),
        out_shape=[jax.ShapeDtypeStruct(shape, jnp.float32) for shape in shapes],
        scratch_shapes=([pltpu.VMEM(proj, jnp.float32)] * 2 if last else [])
        + [
            pltpu.VMEM((4, 512, HALF_IN), jnp.bfloat16),
            pltpu.VMEM((4, 512, HALF_OUT), jnp.bfloat16),
            pltpu.VMEM((4, ROWS, CHUNK), jnp.bfloat16),
            pltpu.SemaphoreType.DMA((4, 12)),
        ],
        compiler_params=pltpu.CompilerParams(vmem_limit_bytes=LIMIT),
        cost_estimate=pl.CostEstimate(
            flops=2 * 512 * ROWS * 4 * CHUNK, bytes_accessed=2 * 768 * 4 * CHUNK, transcendentals=0
        ),
    )(where, *tokens, *first, *second, *extra)


def shards(
    layer_inputs,
    output_grads,
    query_inputs,
    query_grads,
    input_eigen,
    output_eigen,
    doc_index,
    kept_counts,
):
    y, z, xh, xl, core = (lax.axis_index(a) for a in AXES)
    def mixed(of_in, of_out):
        return jnp.concatenate(
            [of_in[..., :HALF_IN], of_out[..., :HALF_OUT], of_in[..., HALF_IN:], of_out[..., HALF_OUT:]], axis=-1
        )

    factors, eigen = mixed(query_inputs[0], query_grads[0]), mixed(input_eigen, output_eigen)
    pre = (factors.astype(jnp.float32) / (eigen + damping)[None, :]).astype(jnp.bfloat16)
    low, high = pre[:4], pre[4:]
    kept = jnp.where(core == 0, low, high)
    came = swap_cores(jnp.where(core == 0, high, low))
    ids_came = swap_cores(doc_index[0])
    both = jnp.where(core == 0, jnp.stack([kept, came], axis=1), jnp.stack([came, kept], axis=1))
    own = both.reshape(8, 2 * CHUNK)

    chip_ids = jnp.where(core == 0, jnp.stack([doc_index[0], ids_came]), jnp.stack([ids_came, doc_index[0]]))
    own, output_grads, chip_ids = lax.optimization_barrier((own, output_grads, chip_ids))
    mate_ids = lax.ppermute(chip_ids, "xl", [(0, 1), (1, 0)])
    g_other = swap_cores(output_grads)
    slots, first_came = gather_z(own)
    first_came, layer_inputs, mate_ids = lax.optimization_barrier((first_came, layer_inputs, mate_ids))
    x_other = swap_cores(layer_inputs)

    halves = [slots[:, :CHUNK].reshape(32, 2 * CHUNK), slots[:, CHUNK:].reshape(32, 2 * CHUNK)]
    halves, x_other, g_other = lax.optimization_barrier((halves, x_other, g_other))

    first, second = direct(halves[0], "y"), direct(halves[1], "x")

    def go_round(one, two, axis):
        pair = [jnp.concatenate([one, two], axis=0)]
        for _ in range(3):
            pair.append(shift(pair[-1], axis, 1, -1))
        return pair

    even_second = go_round(second[0], second[2], "y")
    near_first = go_round(first[0], first[1], "x")
    far_first = go_round(first[2], first[3], "x")
    odd_second = go_round(second[1], second[3], "y")

    ids = jnp.where(xl == 0, jnp.stack([chip_ids, mate_ids]), jnp.stack([mate_ids, chip_ids])).reshape(-1)
    weights = doc_weights(ids, kept_counts[0]).T
    seq = xl * 2 + core
    w_own = lax.dynamic_slice(weights, (seq * 256, 0), (256, DOCS))
    w_other = lax.dynamic_slice(weights, ((seq ^ 1) * 256, 0), (256, DOCS))

    where = jnp.stack([y, z, xh, xl, core]).astype(jnp.int32)
    tokens = (layer_inputs, x_other, output_grads, g_other)
    even = score(where, tokens, [near_first[0], far_first[0], near_first[2], far_first[2]], even_second)
    pieces = score(
        where,
        tokens,
        [near_first[1], far_first[1], near_first[3], far_first[3]],
        odd_second,
        (w_own, w_other, *even),
    )
    total = pieces[0]
    for away in (1, 2, 3):
        total = total + lax.ppermute(pieces[away], ("xl", "core"), [(i, i ^ away) for i in range(4)])
    return total.T


def solution(mesh):
    fine = Mesh(mesh.devices.reshape(NY, NZ, 2, 2, 2), AXES)
    dp, seq = ("y", "z", "xh"), ("xl", "core")
    placed = (
        P(dp + seq, None),
        P(dp + seq, None),
        P(dp, None, seq),
        P(dp, None, seq),
        P(seq),
        P(seq),
        P(dp, seq),
        P(dp, None),
    )
    return jax.shard_map(shards, mesh=fine, in_specs=placed, out_specs=P(seq, dp), check_vma=False)
```

```python
import functools

import jax
import jax.numpy as jnp
from jax import lax
from jax.experimental import pallas as pl
from jax.experimental.pallas import tpu as pltpu
from jax.sharding import Mesh
from jax.sharding import PartitionSpec as P

RANK = 8
DOCS = 8
NY, NZ, NX = 4, 8, 4
AXES = ("y", "z", "xh", "xl", "core")
SIZE = {"y": NY, "z": NZ, "x": NX}
damping = 0.1

ROWS = 256
HALF_IN, OUT = 512, 3584
WIDTHS = 1664, 1920
STARTS = 0, WIDTHS[0]
CHUNKS = HALF_IN + WIDTHS[0], HALF_IN + WIDTHS[1]
NT = (((1,), (1,)), ((), ()))
LIMIT = 32 * 1024 * 1024


def device_at(y, z, x, core):
    return ((y * NZ + z) * NX + x) * 2 + core


def shift(value, axis, step0, step1):
    pairs = []
    for y in range(NY):
        for z in range(NZ):
            for x in range(NX):
                for core in range(2):
                    at = {"y": y, "z": z, "x": x}
                    at[axis] = (at[axis] + (step1 if core else step0)) % SIZE[axis]
                    pairs.append((device_at(y, z, x, core), device_at(at["y"], at["z"], at["x"], core)))
    return lax.ppermute(value, AXES, pairs)


def swap_cores(value):
    return lax.ppermute(value, "core", [(0, 1), (1, 0)])


def direct(own, axis):
    return [own, shift(own, axis, 1, -1), shift(own, axis, 2, -2), shift(own, axis, -1, 1)]


def gather_z(own):
    a = shift(own, "z", 1, -1)
    b = shift(own, "z", -1, 1)
    a2 = shift(own, "z", 2, -2)
    b2 = shift(own, "z", -2, 2)
    c = shift(jnp.concatenate([a, a2], axis=0), "z", 2, -2)
    d = shift(b, "z", -2, 2)
    return jnp.concatenate([own, a, a2, c, d, b2, b], axis=0), a


def doc_weights(row_ids, row_kept):
    positions = jnp.arange(row_ids.shape[0], dtype=jnp.int32)
    onehot = (row_ids[None, :] == jnp.arange(DOCS, dtype=jnp.int32)[:, None]).astype(jnp.int32)
    length = jnp.sum(onehot, axis=1)
    first = jnp.cumsum(length) - length
    used = jnp.minimum(length, row_kept).astype(jnp.float32)
    counted = (positions[None, :] - first[:, None] < row_kept[:, None]).astype(jnp.float32)
    return onehot.astype(jnp.float32) * counted / jnp.sqrt(used)[:, None]


def project(odd, where, tokens, first, second, acc_in, acc_out, xs, gs, ws, sems):
    def copies(piece):
        half, quarter = divmod(piece, 2)
        at = (where[3] ^ odd) * 2 + quarter
        width, chunk = WIDTHS[half], CHUNKS[half]
        of_x = pl.ds(pl.multiple_of(at * 2 * HALF_IN + half * HALF_IN, 128), HALF_IN)
        of_g = pl.ds(pl.multiple_of(at * OUT + STARTS[half], 128), width)
        of_w = pl.ds(quarter * chunk, chunk)
        to_g, to_w = pl.ds(0, width), pl.ds(0, chunk)
        x_own, x_other, g_own, g_other = tokens
        moves = [
            (x_own.at[:, of_x], xs.at[piece, pl.ds(0, 256)]),
            (x_other.at[:, of_x], xs.at[piece, pl.ds(256, 256)]),
            (g_own.at[:, of_g], gs.at[piece, pl.ds(0, 256), to_g]),
            (g_other.at[:, of_g], gs.at[piece, pl.ds(256, 256), to_g]),
        ]
        if half == 0:
            moves += [(v.at[:, of_w], ws.at[piece, pl.ds(64 * i, 64), to_w]) for i, v in enumerate(first)]
        else:
            moves += [
                (second[y].at[pl.ds(32 * k, 32), of_w], ws.at[piece, pl.ds(128 * k + 32 * y, 32), to_w])
                for k in range(2)
                for y in range(4)
            ]
        return [pltpu.make_async_copy(src, dst, sems.at[piece, i]) for i, (src, dst) in enumerate(moves)]

    for piece in range(4):
        for copy in copies(piece):
            copy.start()
    for piece in range(4):
        for copy in copies(piece):
            copy.wait()
        p = lax.dot_general(xs[piece], ws[piece, :, :HALF_IN], NT, preferred_element_type=jnp.float32)
        width, chunk = WIDTHS[piece // 2], CHUNKS[piece // 2]
        q = lax.dot_general(
            gs[piece, :, :width], ws[piece, :, HALF_IN:chunk], NT, preferred_element_type=jnp.float32
        )
        if piece == 0:
            acc_in[...] = p
            acc_out[...] = q
        else:
            acc_in[...] += p
            acc_out[...] += q


def even_kernel(where, *refs):
    project(0, where, refs[:4], refs[4:8], refs[8:12], *refs[12:])


def odd_kernel(where, *refs):
    w_own, w_other, even_in, even_out = refs[12:16]
    outs, (acc_in, acc_out, *scratch) = refs[16:20], refs[20:]
    project(1, where, refs[:4], refs[4:8], refs[8:12], acc_in, acc_out, *scratch)
    y, z, xh, xl, core = (where[i] for i in range(5))
    swapped = xl == core

    def total(even, acc):
        odd = acc[...]
        turned = jnp.concatenate([odd[:, 128:], odd[:, :128]], axis=1)
        return even[...] + jnp.where(swapped, turned, odd)

    prod = total(even_in, acc_in) * total(even_out, acc_out)
    own_prod, other_prod = prod[:256], prod[256:]
    by_doc = []
    for doc in range(DOCS):
        weighted = own_prod * w_own[:, doc : doc + 1] + other_prod * w_other[:, doc : doc + 1]
        by_doc.append(jnp.sum(weighted, axis=0, keepdims=True))
    sums = jnp.concatenate(by_doc, axis=0)
    row = lax.broadcasted_iota(jnp.int32, (64, ROWS), 1)
    slot = lax.broadcasted_iota(jnp.int32, (64, ROWS), 0)
    sign = 2 * core - 1
    row_z = (z + sign * ((row >> 2) & 7)) & 7
    row_y = (y + sign * ((row >> 5) & 3)) & 3
    row_xh = xh ^ (row >> 7)
    row_query = (row_y * 8 + row_z) * 2 + row_xh
    seq = xl * 2 + core
    pick = (row_query == (seq ^ (slot >> 4)) * 16 + (slot & 15)).astype(jnp.float32).astype(jnp.bfloat16)
    top = sums.astype(jnp.bfloat16)
    rest = sums - top.astype(jnp.float32)
    middle = rest.astype(jnp.bfloat16)
    low = (rest - middle.astype(jnp.float32)).astype(jnp.bfloat16)
    picked = sum(
        lax.dot_general(part, pick, NT, preferred_element_type=jnp.float32) for part in (low, middle, top)
    )
    for away in range(4):
        outs[away][...] = picked[:, 16 * away : 16 * away + 16]


def score(where, tokens, first, second, extra=()):
    last = bool(extra)
    proj = (512, ROWS)
    vmem = pl.BlockSpec(memory_space=pltpu.VMEM)
    shapes = [(DOCS, 16)] * 4 if last else [proj] * 2
    return pl.pallas_call(
        odd_kernel if last else even_kernel,
        in_specs=[pl.BlockSpec(memory_space=pltpu.SMEM)]
        + [pl.BlockSpec(memory_space=pl.ANY)] * 12
        + [vmem] * len(extra),
        out_specs=[vmem] * len(shapes),
        out_shape=[jax.ShapeDtypeStruct(shape, jnp.float32) for shape in shapes],
        scratch_shapes=([pltpu.VMEM(proj, jnp.float32)] * 2 if last else [])
        + [
            pltpu.VMEM((4, 512, HALF_IN), jnp.bfloat16),
            pltpu.VMEM((4, 512, max(WIDTHS)), jnp.bfloat16),
            pltpu.VMEM((4, ROWS, max(CHUNKS)), jnp.bfloat16),
            pltpu.SemaphoreType.DMA((4, 12)),
        ],
        compiler_params=pltpu.CompilerParams(vmem_limit_bytes=LIMIT),
        cost_estimate=pl.CostEstimate(
            flops=2 * 512 * ROWS * 2 * sum(CHUNKS), bytes_accessed=2 * 768 * 2 * sum(CHUNKS), transcendentals=0
        ),
    )(where, *tokens, *first, *second, *extra)


def shards(
    layer_inputs,
    output_grads,
    query_inputs,
    query_grads,
    input_eigen,
    output_eigen,
    doc_index,
    kept_counts,
):
    y, z, xh, xl, core = (lax.axis_index(a) for a in AXES)
    def mixed(of_in, of_out):
        return jnp.concatenate(
            [of_in[..., :HALF_IN], of_out[..., : WIDTHS[0]], of_in[..., HALF_IN:], of_out[..., WIDTHS[0] :]], axis=-1
        )

    factors, eigen = mixed(query_inputs[0], query_grads[0]), mixed(input_eigen, output_eigen)
    pre = (factors.astype(jnp.float32) / (eigen + damping)[None, :]).astype(jnp.bfloat16)
    low, high = pre[:4], pre[4:]
    kept = jnp.where(core == 0, low, high)
    came = swap_cores(jnp.where(core == 0, high, low))
    ids_came = swap_cores(doc_index[0])
    both = jnp.where(core == 0, jnp.stack([kept, came], axis=1), jnp.stack([came, kept], axis=1))
    own = both.reshape(8, sum(CHUNKS))

    chip_ids = jnp.where(core == 0, jnp.stack([doc_index[0], ids_came]), jnp.stack([ids_came, doc_index[0]]))
    own, output_grads, chip_ids = lax.optimization_barrier((own, output_grads, chip_ids))
    mate_ids = lax.ppermute(chip_ids, "xl", [(0, 1), (1, 0)])
    g_other = swap_cores(output_grads)
    slots, first_came = gather_z(own)
    first_came, layer_inputs, mate_ids = lax.optimization_barrier((first_came, layer_inputs, mate_ids))
    x_other = swap_cores(layer_inputs)

    halves = [slots[:, : CHUNKS[0]].reshape(32, 2 * CHUNKS[0]), slots[:, CHUNKS[0] :].reshape(32, 2 * CHUNKS[1])]
    halves, x_other, g_other = lax.optimization_barrier((halves, x_other, g_other))

    first, second = direct(halves[0], "y"), direct(halves[1], "x")

    def go_round(one, two, axis):
        pair = [jnp.concatenate([one, two], axis=0)]
        for _ in range(3):
            pair.append(shift(pair[-1], axis, 1, -1))
        return pair

    even_second = go_round(second[0], second[2], "y")
    near_first = go_round(first[0], first[1], "x")
    far_first = go_round(first[2], first[3], "x")
    odd_second = go_round(second[1], second[3], "y")

    ids = jnp.where(xl == 0, jnp.stack([chip_ids, mate_ids]), jnp.stack([mate_ids, chip_ids])).reshape(-1)
    weights = doc_weights(ids, kept_counts[0]).T
    seq = xl * 2 + core
    w_own = lax.dynamic_slice(weights, (seq * 256, 0), (256, DOCS))
    w_other = lax.dynamic_slice(weights, ((seq ^ 1) * 256, 0), (256, DOCS))

    where = jnp.stack([y, z, xh, xl, core]).astype(jnp.int32)
    tokens = (layer_inputs, x_other, output_grads, g_other)
    even = score(where, tokens, [near_first[0], far_first[0], near_first[2], far_first[2]], even_second)
    pieces = score(
        where,
        tokens,
        [near_first[1], far_first[1], near_first[3], far_first[3]],
        odd_second,
        (w_own, w_other, *even),
    )
    total = pieces[0]
    for away in (1, 2, 3):
        total = total + lax.ppermute(pieces[away], ("xl", "core"), [(i, i ^ away) for i in range(4)])
    return total.T


def solution(mesh):
    fine = Mesh(mesh.devices.reshape(NY, NZ, 2, 2, 2), AXES)
    dp, seq = ("y", "z", "xh"), ("xl", "core")
    placed = (
        P(dp + seq, None),
        P(dp + seq, None),
        P(dp, None, seq),
        P(dp, None, seq),
        P(seq),
        P(seq),
        P(dp, seq),
        P(dp, None),
    )
    return jax.shard_map(shards, mesh=fine, in_specs=placed, out_specs=P(seq, dp), check_vma=False)
```
